128 devices in a mesh: ctx: 32 (over x, z_lo, y), head: 4 (over z_hi, core).
Axes of the slice: x: 4, y: 4, z: 4 (z_hi: 2, z_lo: 2; z = z_hi * 2 + z_lo), core: 2. Of those that a mesh axis runs over, the one named last changes fastest.
Arguments:
- query_states: bfloat16 [512, 8192], P(None, 'ctx'), may hold values from -40 to 40
- key_states: bfloat16 [24576, 8192], P('ctx'), may hold values from -40 to 40
- w_query: bfloat16 [8192, 8192], P('ctx', 'head'), may hold values from -2 to 2
- w_key: bfloat16 [8192, 1024], P(None, 'head'), may hold values from -1 to 1
- w_value: bfloat16 [8192, 1024], P(None, 'head'), may hold values from -0.0625 to 0.0625
- w_out: bfloat16 [8192, 8192], P('head', 'ctx'), may hold values from -2 to 2
- slab_start: int32 [1], replicated, may hold values from 12288 to 24064
Outputs:
- flow_map: float32 [512, 24576], P('head', 'ctx')
The draws below stay inside these ranges and needn't reach their ends.
All inputs are finite; a program needn't handle non-finite values.
Results may differ from the reference program's by a relative error of at most 0.0033.
The reference program's roundings to bfloat16 on the way (of `queries`) count: a program that leaves them out, or rounds other values in their place, can miss the bound.
Values may be sent and summed in bfloat16 or wider, within the bound.
No kernel may reach another device: no remote copies, remote signals or barrier semaphores. Data moves between devices by JAX's collectives and lax.ppermute only.
A program may use at most 128 MiB of HBM per device.

```python
import math
import jax
import jax.numpy as jnp
from jax import lax

D = 8192
HEADS = 64
KV_HEADS = 8
HEAD_DIM = 128
Q = 512
KEYS = 24576


def shared_keys(key):
    base_rows = jax.random.normal(jax.random.fold_in(key, 11), (KEYS, D), jnp.float32)
    row_scale = jnp.exp(jax.random.uniform(jax.random.fold_in(key, 12), (KEYS, 1), jnp.float32, minval=math.log(0.5), maxval=math.log(5.0)))
    states = base_rows * row_scale
    return states


def shared_wkey(key):
    return jax.random.normal(jax.random.fold_in(key, 21), (D, KV_HEADS * HEAD_DIM), jnp.float32) / math.sqrt(D)


def draw_key_states(key, part):
    return shared_keys(key).astype(jnp.bfloat16)


def draw_query_states(key, part):
    states = jax.random.normal(jax.random.fold_in(key, 41), (Q, D), jnp.float32)
    return states.astype(jnp.bfloat16)


def draw_w_key(key, part):
    return shared_wkey(key).astype(jnp.bfloat16)


def draw_w_query(key, part):
    noise = jax.random.normal(jax.random.fold_in(key, 31), (D, HEADS * HEAD_DIM), jnp.float32) / math.sqrt(D)
    weights = noise
    return weights.astype(jnp.bfloat16)


def draw_w_out(key, part):
    key = jax.random.fold_in(key, 51)
    block_shape = (HEADS, HEAD_DIM, D)
    noise = jnp.clip(jax.random.normal(jax.random.fold_in(key, 1), block_shape, jnp.float32), -4.0, 4.0)
    coefs = jnp.clip(jax.random.normal(jax.random.fold_in(key, 2), (HEADS, HEAD_DIM, 4), jnp.float32), -4.0, 4.0)
    directions = jnp.clip(jax.random.normal(jax.random.fold_in(key, 3), (HEADS, 4, D), jnp.float32), -4.0, 4.0)
    weights = noise
    for column in range(4):
        weights = weights + coefs[:, :, column:column + 1] * directions[:, column:column + 1, :]
    head_scale = jnp.exp(jax.random.uniform(jax.random.fold_in(key, 4), (HEADS, 1, 1), jnp.float32, minval=math.log(0.5), maxval=math.log(2.0)))
    weights = weights * head_scale / math.sqrt(5.0 * HEADS * HEAD_DIM)
    weights = jnp.clip(weights, -2.0, 2.0)
    return weights.reshape(HEADS * HEAD_DIM, D).astype(jnp.bfloat16)


def level_of(key, extent, cuts, least, largest):
    factor_of = 1.0
    for axis_at, blocks in cuts:
        heights = jax.random.uniform(jax.random.fold_in(jax.random.fold_in(key, 6), axis_at), (blocks,), jnp.float32, least / len(cuts), largest / len(cuts))
        factor_of = factor_of * jnp.repeat(jnp.exp(heights), extent[axis_at] // blocks).reshape((-1,) + (1,) * (len(extent) - 1 - axis_at))
    return factor_of


def gaussian(rng, dims, deviation, reach, pieces=(), kind=jnp.bfloat16):
    values = deviation * jax.random.normal(rng, dims, jnp.float32)
    if pieces:
        values = values * level_of(rng, dims, pieces, -0.22, 0.18)
    return jnp.clip(values, -reach, reach).astype(kind)


def setup_inputs(seed: int = 0) -> dict:
    key_list = jax.random.split(jax.random.key(seed), 8)
    query_states = draw_query_states(jax.random.fold_in(key_list[7], 71), 0)
    key_states = draw_key_states(jax.random.fold_in(key_list[7], 71), 0)
    w_query = draw_w_query(jax.random.fold_in(key_list[7], 71), 0)
    w_key = draw_w_key(jax.random.fold_in(key_list[7], 71), 0)
    w_value = gaussian(key_list[4], (D, KV_HEADS * HEAD_DIM), D ** -0.5, 0.0625, ((1, 4),))
    w_out = draw_w_out(jax.random.fold_in(key_list[7], 71), 0)
    slab_start = jax.random.randint(key_list[6], (1,), KEYS // 2, KEYS - Q + 1).astype(jnp.int32)
    return dict(query_states=query_states, key_states=key_states, w_query=w_query, w_key=w_key, w_value=w_value, w_out=w_out, slab_start=slab_start)


masked_value = -1e+30

def reference(query_states, key_states, w_query, w_key, w_value, w_out, slab_start):
    group_size = HEADS // KV_HEADS
    queries = jnp.dot(query_states, w_query, preferred_element_type=jnp.float32).astype(jnp.bfloat16).reshape(Q, HEADS, HEAD_DIM)
    key_proj = jnp.dot(key_states, w_key, preferred_element_type=jnp.float32).astype(jnp.bfloat16).reshape(KEYS, KV_HEADS, HEAD_DIM)
    value_proj = jnp.dot(key_states, w_value, preferred_element_type=jnp.float32).astype(jnp.bfloat16).reshape(KEYS, KV_HEADS, HEAD_DIM)
    out_blocks = w_out.reshape(HEADS, HEAD_DIM, D)
    slab_first = slab_start[0]
    query_pos = slab_first + jnp.arange(Q, dtype=jnp.int32)
    key_pos = jnp.arange(KEYS, dtype=jnp.int32)
    visible = key_pos[None, :] <= query_pos[:, None]
    scale_factor = HEAD_DIM ** (-0.5)

    def per_head(running, head_idx):
        group_idx = head_idx // group_size
        query_head = lax.dynamic_index_in_dim(queries, head_idx, 1, keepdims=False)
        key_head = lax.dynamic_index_in_dim(key_proj, group_idx, 1, keepdims=False)
        value_head = lax.dynamic_index_in_dim(value_proj, group_idx, 1, keepdims=False)
        out_head = lax.dynamic_index_in_dim(out_blocks, head_idx, 0, keepdims=False)
        gram_mat = jnp.dot(out_head, out_head.T, preferred_element_type=jnp.float32)
        value_f32 = value_head.astype(jnp.float32)
        projected = jnp.dot(value_f32, gram_mat, precision=lax.Precision.HIGHEST)
        value_norm = jnp.sqrt(lax.optimization_barrier(jnp.sum(projected * value_f32, axis=1)) + 1e-06)
        scores = jnp.dot(query_head, key_head.T, preferred_element_type=jnp.float32) * scale_factor
        scores = jnp.where(visible, scores, masked_value)
        peak = lax.optimization_barrier(jnp.max(scores, axis=1, keepdims=True))
        exp_terms = jnp.where(visible, jnp.exp(scores - peak), 0.0)
        denom_sum = lax.optimization_barrier(jnp.sum(exp_terms, axis=1, keepdims=True))
        return (running + exp_terms / denom_sum * value_norm[None, :], None)
    contrib, unused = lax.scan(per_head, jnp.zeros((Q, KEYS), jnp.float32), jnp.arange(HEADS, dtype=jnp.int32))
    total = lax.optimization_barrier(jnp.sum(contrib, axis=1, keepdims=True))
    row_pos = (query_pos[:, None] + 1).astype(jnp.float32)
    return row_pos * contrib / total
```

```python
import jax
import jax.numpy as jnp
from jax import lax
from jax.experimental import pallas as pl
from jax.experimental.pallas import tpu as pltpu
from jax.sharding import Mesh, PartitionSpec as P

HEAD_DIM = 128
LOG2E = 1.4426950408889634
MASKED = -1e30
NX, NZ, NY, NH, NC = 4, 2, 4, 2, 2
XZ, CTX, MAP = ("x", "zl"), ("x", "zl", "y"), ("y", "zh", "core")
F32, BF16 = jnp.float32, jnp.bfloat16
VMEM_LIMIT = 56 * 1024 * 1024


def nn(a, b):
    return lax.dot_general(a, b, (((1,), (0,)), ((), ())), preferred_element_type=F32)


def nt(a, b):
    return lax.dot_general(a, b, (((1,), (1,)), ((), ())), preferred_element_type=F32)


def partial_kernel(got_ref, out_ref):
    for c in range(2):
        acc = jnp.zeros((512, 256), F32)
        for s in range(4):
            acc += nn(got_ref[s, 512:1024, :], got_ref[s, c * 256:(c + 1) * 256, :])
        out_ref[:, :, c * 256:(c + 1) * 256] = acc.reshape(8, 64, 256)
    for h in range(4):
        gram = jnp.zeros((128, 128), F32)
        for s in range(4):
            rows = got_ref[s, 1024 + h * 128:1024 + (h + 1) * 128, :]
            gram += nt(rows, rows)
        out_ref[2 * h, :, 512:640] = gram[:64]
        out_ref[2 * h + 1, :, 512:640] = gram[64:]


def scores_kernel(info_ref, q_ref, g_ref, *refs):
    k_refs, v_refs = refs[0:4], refs[4:8]
    p_ref, stat_ref, s_scr, acc_scr = refs[8:12]
    h = pl.program_id(0)
    slab, y, key0 = info_ref[0], info_ref[1], info_ref[2]
    q = q_ref[:, 0].reshape(128, 128)
    gram = jnp.concatenate(
        [g_ref[half, 0, :, b * 128:(b + 1) * 128] for half in range(2) for b in range(4)], axis=0
    )
    row = lax.broadcasted_iota(jnp.int32, (128, 1), 0)
    q_pos = slab + (row // 32) * 128 + y * 32 + row % 32
    lane = lax.broadcasted_iota(jnp.int32, (128, 768), 1)
    peak = jnp.full((128, 1), MASKED, F32)
    for s in range(4):
        first = key0 + ((y + s) % 4) * 768
        scores = nn(q, k_refs[s][...]) * (HEAD_DIM ** -0.5 * LOG2E)
        scores = jnp.where(lane <= q_pos - first, scores, MASKED)
        s_scr[s] = scores
        peak = jnp.maximum(peak, jnp.max(scores, axis=1, keepdims=True))
    e_sum = jnp.zeros((128, 1), F32)
    t_sum = jnp.zeros((128, 1), F32)
    for s in range(4):
        v = v_refs[s][...]
        quad = jnp.sum(nn(gram, v) * v.astype(F32), axis=0, keepdims=True)
        norm = jnp.sqrt(jnp.maximum(quad, 0.0) + 1e-6)
        e = jnp.exp2(s_scr[s] - peak)
        p = e * norm
        e_sum += jnp.sum(e, axis=1, keepdims=True)
        t_sum += jnp.sum(p, axis=1, keepdims=True)
        p_ref[0, s] = p.astype(BF16)
    at = lax.broadcasted_iota(jnp.int32, (128, 128), 1)
    acc = jnp.where(at == h, peak, acc_scr[...])
    acc = jnp.where(at == h + 16, e_sum, acc)
    acc = jnp.where(at == h + 32, t_sum, acc)
    acc_scr[...] = acc

    @pl.when(h == pl.num_programs(0) - 1)
    def _():
        stat_ref[...] = acc.T[:48]


def map_kernel(info_ref, p_ref, own_ref, all_ref, out_ref, w_scr):
    @pl.when(pl.program_id(0) == 0)
    def _():
        peaks = all_ref[:, 0:16, :]
        peak = jnp.max(peaks, axis=0)
        factor = jnp.exp2(peaks - peak[None])
        denom = jnp.sum(all_ref[:, 16:32, :] * factor, axis=0)
        part = jnp.sum(all_ref[:, 32:48, :] * factor, axis=0)
        weight = jnp.exp2(own_ref[0:16, :] - peak) / denom
        total = jnp.sum(part / denom, axis=0, keepdims=True)
        w_scr[...] = jnp.concatenate(
            [weight, total, jnp.zeros((111, 128), F32)], axis=0
        ).T

    acc = jnp.zeros((128, 768), F32)
    for h in range(16):
        acc += p_ref[h, 0].astype(F32) * w_scr[:, h:h + 1]
    out_ref[0, :, 0:768] = acc.astype(BF16)
    total = w_scr[:, 16:17]
    hi = total.astype(BF16).astype(F32)
    lane = lax.broadcasted_iota(jnp.int32, (128, 128), 1)
    out_ref[0, :, 768:896] = jnp.where(
        lane == 0, hi, jnp.where(lane == 1, total - hi, 0.0)
    ).astype(BF16)


def final_kernel(info_ref, got_ref, out_ref):
    slab, head = info_ref[0], info_ref[3]
    for y in range(4):
        rows = got_ref[4 * y].astype(F32)
        for h in range(1, 4):
            rows += got_ref[4 * y + h].astype(F32)
        total = rows[:, 768:769] + rows[:, 769:770]
        row = lax.broadcasted_iota(jnp.int32, (32, 1), 0)
        pos = (slab + head * 128 + y * 32 + row + 1).astype(F32)
        out_ref[y * 32:(y + 1) * 32, :] = rows[:, :768] * (pos / total)


def local(query_states, key_states, w_query, w_key, w_value, w_out, slab_start):
    x, zl, y = lax.axis_index("x"), lax.axis_index("zl"), lax.axis_index("y")
    head = lax.axis_index("zh") * NC + lax.axis_index("core")
    xz = x * NZ + zl
    info = jnp.stack([slab_start[0], y, xz * 3072, head]).astype(jnp.int32)

    rows = query_states.reshape(4, 4, 2, 16, 256).transpose(0, 2, 1, 3, 4).reshape(1, 512, 256)
    columns = w_query.reshape(256, 4, 2, 256).transpose(1, 2, 0, 3).reshape(4, 512, 256)
    pay = jnp.concatenate(
        [columns, jnp.broadcast_to(rows, (4, 512, 256)), w_out.reshape(4, 512, 256)], axis=1
    )
    got = lax.all_to_all(pay, "y", 0, 0, tiled=True)
    parts = pl.pallas_call(
        partial_kernel,
        out_shape=jax.ShapeDtypeStruct((8, 64, 640), F32),
        in_specs=[pl.BlockSpec(memory_space=pltpu.VMEM)],
        out_specs=pl.BlockSpec(memory_space=pltpu.VMEM),
        compiler_params=pltpu.CompilerParams(vmem_limit_bytes=VMEM_LIMIT),
        name="partial",
    )(got)
    parts = lax.all_to_all(parts, XZ, 0, 0, tiled=True)
    summed = jnp.sum(parts, axis=0).astype(BF16)
    queries = summed[:, :512].reshape(4, 16, 512)
    gram = summed[:, 512:].reshape(4, 16, 128).transpose(1, 0, 2).reshape(1, 16, 512)
    block = jnp.concatenate([queries, jnp.broadcast_to(gram, (4, 16, 512))], axis=1)
    block = jnp.broadcast_to(block[None], (8, 4, 32, 512)).reshape(32, 32, 512)
    block = lax.all_to_all(block, CTX, 0, 0, tiled=True).reshape(8, 4, 32, 512)

    w_kv = jnp.concatenate([w_key, w_value], axis=1)
    own_kv = lax.dot_general(
        w_kv, key_states, (((0,), (1,)), ((), ())), preferred_element_type=F32
    ).astype(BF16)
    kv = [own_kv] + [
        lax.ppermute(own_kv, "y", [(i, (i - s) % NY) for i in range(NY)]) for s in (1, 2, 3)
    ]

    p, stats = pl.pallas_call(
        scores_kernel,
        out_shape=(
            jax.ShapeDtypeStruct((16, 4, 128, 768), BF16),
            jax.ShapeDtypeStruct((48, 128), F32),
        ),
        grid_spec=pltpu.PrefetchScalarGridSpec(
            num_scalar_prefetch=1,
            grid=(16,),
            in_specs=[
                pl.BlockSpec((8, 1, 16, 128), lambda h, i: (0, h // 4, 0, h % 4)),
                pl.BlockSpec((2, 1, 16, 512), lambda h, i: (h % 4, h // 4, 1, 0)),
            ]
            + [pl.BlockSpec((128, 768), lambda h, i: (h // 8, 0))] * 4
            + [pl.BlockSpec((128, 768), lambda h, i: (2 + h // 8, 0))] * 4,
            out_specs=(
                pl.BlockSpec((1, 4, 128, 768), lambda h, i: (h, 0, 0, 0)),
                pl.BlockSpec((48, 128), lambda h, i: (0, 0)),
            ),
            scratch_shapes=[pltpu.VMEM((4, 128, 768), F32), pltpu.VMEM((128, 128), F32)],
        ),
        compiler_params=pltpu.CompilerParams(vmem_limit_bytes=VMEM_LIMIT),
        name="scores",
    )(info, block, block, *kv, *kv)

    all_stats = lax.all_to_all(
        jnp.broadcast_to(stats[None], (8, 48, 128)), XZ, 0, 0, tiled=True
    )

    pay = pl.pallas_call(
        map_kernel,
        out_shape=jax.ShapeDtypeStruct((4, 128, 896), BF16),
        grid_spec=pltpu.PrefetchScalarGridSpec(
            num_scalar_prefetch=1,
            grid=(4,),
            in_specs=[
                pl.BlockSpec((16, 1, 128, 768), lambda s, i: (0, s, 0, 0)),
                pl.BlockSpec((48, 128), lambda s, i: (0, 0)),
                pl.BlockSpec((8, 48, 128), lambda s, i: (0, 0, 0)),
            ],
            out_specs=pl.BlockSpec((1, 128, 896), lambda s, i: ((i[1] + s) % 4, 0, 0)),
            scratch_shapes=[pltpu.VMEM((128, 128), F32)],
        ),
        compiler_params=pltpu.CompilerParams(vmem_limit_bytes=VMEM_LIMIT),
        name="weigh",
    )(info, p, stats, all_stats)
    got = lax.all_to_all(pay.reshape(16, 32, 896), MAP, 0, 0, tiled=True)

    return pl.pallas_call(
        final_kernel,
        out_shape=jax.ShapeDtypeStruct((128, 768), F32),
        in_specs=[
            pl.BlockSpec(memory_space=pltpu.SMEM),
            pl.BlockSpec(memory_space=pltpu.VMEM),
        ],
        out_specs=pl.BlockSpec(memory_space=pltpu.VMEM),
        compiler_params=pltpu.CompilerParams(vmem_limit_bytes=VMEM_LIMIT),
        name="finish",
    )(info, got)


def solution(mesh):
    fine = Mesh(
        mesh.devices.reshape(NX, NZ, NY, NH, NC), ("x", "zl", "y", "zh", "core")
    )
    head = ("zh", "core")
    return jax.shard_map(
        local,
        mesh=fine,
        in_specs=(
            P(None, CTX),
            P(CTX, None),
            P(CTX, head),
            P(None, head),
            P(None, head),
            P(head, CTX),
            P(),
        ),
        out_specs=P(head, CTX),
        check_vma=False,
    )
```

```python
import jax
import jax.numpy as jnp
from jax import lax
from jax.experimental import pallas as pl
from jax.experimental.pallas import tpu as pltpu
from jax.sharding import Mesh, PartitionSpec as P

HEAD_DIM = 128
LOG2E = 1.4426950408889634
MASKED = -1e30
SCALE = HEAD_DIM ** -0.5 * LOG2E
NX, NZ, NY, NH, NC = 4, 2, 4, 2, 2
XZ, ZY, CTX, MAP = ("x", "zl"), ("zl", "y"), ("x", "zl", "y"), ("x", "zh", "core")
F32, BF16 = jnp.float32, jnp.bfloat16
VMEM_LIMIT = 56 * 1024 * 1024


def nn(a, b):
    return lax.dot_general(a, b, (((1,), (0,)), ((), ())), preferred_element_type=F32)


def nt(a, b):
    return lax.dot_general(a, b, (((1,), (1,)), ((), ())), preferred_element_type=F32)


def pack_kernel(wq_ref, qs_ref, wo_ref, out_ref):
    out_ref[0, 0:256, :] = wq_ref[:, 0:256]
    out_ref[0, 256:512, :] = wq_ref[:, 256:512]
    for block in range(4):
        for part in range(4):
            for half in range(2):
                src = ((block * 4 + part) * 2 + half) * 16
                dst = 512 + ((block * 2 + half) * 4 + part) * 16
                out_ref[0, dst:dst + 16, :] = qs_ref[src:src + 16, :]
    for h in range(4):
        rows = wo_ref[h * 128:(h + 1) * 128, :]
        at = 1024 + (h // 2) * 128
        out_ref[0, at:at + 128, (h % 2) * 128:(h % 2 + 1) * 128] = nt(rows, rows).astype(BF16)


def partial_kernel(got_ref, out_ref):
    for c in range(2):
        acc = jnp.zeros((512, 256), F32)
        for s in range(4):
            acc += nn(got_ref[s, 512:1024, :], got_ref[s, c * 256:(c + 1) * 256, :])
        out_ref[:, :, c * 256:(c + 1) * 256] = acc.reshape(8, 64, 256)
    for pair in range(2):
        gram = jnp.zeros((128, 256), F32)
        for s in range(4):
            gram += got_ref[s, 1024 + pair * 128:1024 + (pair + 1) * 128, :].astype(F32)
        for k in range(2):
            h = 2 * pair + k
            out_ref[2 * h, :, 512:640] = gram[:64, k * 128:(k + 1) * 128]
            out_ref[2 * h + 1, :, 512:640] = gram[64:, k * 128:(k + 1) * 128]


def sum_kernel(got_ref, out_ref):
    total = got_ref[0]
    for k in range(1, 8):
        total += got_ref[k]
    total = total.astype(BF16)
    gram = jnp.concatenate([total[b * 16:(b + 1) * 16, 512:640] for b in range(4)], axis=1)
    for part in range(4):
        for k in range(8):
            out_ref[part, k, 0:16, :] = total[part * 16:(part + 1) * 16, 0:512]
            out_ref[part, k, 16:32, :] = gram


def kv_kernel(k_ref, wk_ref, wv_ref, key_ref, value_ref, acc):
    i = pl.program_id(0)
    k = k_ref[...]
    part = jnp.concatenate([nn(k, wk_ref[...]), nn(k, wv_ref[...])], axis=1)

    @pl.when(i == 0)
    def _():
        acc[...] = part

    @pl.when(i > 0)
    def _():
        acc[...] += part

    @pl.when(i == pl.num_programs(0) - 1)
    def _():
        turned = acc[...].T.astype(BF16)
        key_ref[...] = turned[:256]
        value_ref[...] = turned[256:]


def norm_kernel(value_ref, block_ref, out_ref):
    for h in range(16):
        gram = jnp.concatenate(
            [
                block_ref[2 * (h % 4) + half, h // 4, 16:32, b * 128:(b + 1) * 128]
                for half in range(2)
                for b in range(4)
            ],
            axis=0,
        )
        v = value_ref[(h // 8) * 128:(h // 8 + 1) * 128, :]
        quad = jnp.sum(nn(gram, v) * v.astype(F32), axis=0, keepdims=True)
        out_ref[h // 4, h % 4:h % 4 + 1, :] = jnp.sqrt(jnp.maximum(quad, 0.0) + 1e-6)


def tile_first(info_ref, s):
    return (((info_ref[1] + s) % 4) * 8 + info_ref[2]) * 768


def last_row(info_ref):
    return info_ref[0] + info_ref[1] * 32 + 3 * 128 + 31


def score_tiles(info_ref, q_ref, keys, norms, p_ref, acc, tiles):
    j = pl.program_id(0)
    slab, me = info_ref[0], info_ref[1]
    at = lax.broadcasted_iota(jnp.int32, (128, 128), 1)

    def scored(n, first, masked):
        k = keys[n][...]
        stat = acc[n]
        if masked:
            row = lax.broadcasted_iota(jnp.int32, (128, 1), 0)
            q_pos = slab + (row // 32) * 128 + me * 32 + row % 32
            seen = lax.broadcasted_iota(jnp.int32, (128, 768), 1) <= q_pos - first
        for i in range(4):
            q = q_ref[:, 0, :, i * 128:(i + 1) * 128].reshape(128, 128)
            scores = nn(q, k)
            if masked:
                scores = jnp.where(seen, scores, MASKED)
            peak = jnp.max(scores, axis=1, keepdims=True) * SCALE
            e = jnp.exp2(scores * SCALE - peak)
            p = e * norms[n][0, i:i + 1, :]
            h = 4 * j + i
            stat = jnp.where(at == h, peak, stat)
            stat = jnp.where(at == h + 16, jnp.sum(e, axis=1, keepdims=True), stat)
            stat = jnp.where(at == h + 32, jnp.sum(p, axis=1, keepdims=True), stat)
            p_ref[i, n] = p.astype(BF16)
        acc[n] = stat

    for n, s in enumerate(tiles):
        first = tile_first(info_ref, s)
        full = first + 767 <= slab + me * 32
        none = first > last_row(info_ref)

        @pl.when(full)
        def _():
            scored(n, first, False)

        @pl.when(jnp.logical_not(full) & jnp.logical_not(none))
        def _():
            scored(n, first, True)

        @pl.when(none)
        def _():
            acc[n] = jnp.where(at < 16, MASKED, 0.0)


def own_kernel(info_ref, q_ref, key_ref, norm_ref, p_ref, stat_ref, acc):
    score_tiles(info_ref, q_ref, [key_ref], [norm_ref], p_ref, acc, (0,))

    @pl.when(pl.program_id(0) == 3)
    def _():
        stat_ref[...] = acc[0].T[:48]


def other_kernel(info_ref, q_ref, own_ref, *refs):
    p_ref, stat_ref, peak_ref, acc = refs[6:]
    score_tiles(info_ref, q_ref, refs[0:3], refs[3:6], p_ref, acc, (1, 2, 3))

    @pl.when(pl.program_id(0) == 3)
    def _():
        stats = jnp.stack([own_ref[...]] + [acc[n].T[:48] for n in range(3)])
        peaks = stats[:, 0:16]
        peak = jnp.max(peaks, axis=0)
        factor = jnp.exp2(peaks - peak[None])
        denom = jnp.sum(stats[:, 16:32] * factor, axis=0)
        part = jnp.sum(stats[:, 32:48] * factor, axis=0)
        merged = jnp.concatenate([peak, denom, part], axis=0)
        stat_ref[...] = jnp.broadcast_to(merged[None], (8, 48, 128))
        peak_ref[...] = peaks


def map_kernel(info_ref, own_p_ref, p_ref, peak_ref, all_ref, out_ref, buf, w_scr, sems):
    seen = [tile_first(info_ref, s) <= last_row(info_ref) for s in range(4)]

    def copy(s, part):
        heads = pl.ds(part * 4, 4)
        src = own_p_ref.at[heads, 0] if s == 0 else p_ref.at[heads, s - 1]
        return pltpu.make_async_copy(src, buf.at[s, heads], sems.at[s, part])

    for s in range(4):
        @pl.when(seen[s])
        def _():
            for part in range(4):
                copy(s, part).start()

    peaks = all_ref[:, 0:16, :]
    peak = jnp.max(peaks, axis=0)
    factor = jnp.exp2(peaks - peak[None])
    denom = jnp.sum(all_ref[:, 16:32, :] * factor, axis=0)
    part_sum = jnp.sum(all_ref[:, 32:48, :] * factor, axis=0)
    total = jnp.sum(part_sum / denom, axis=0, keepdims=True)
    for n in range(4):
        weight = jnp.exp2(peak_ref[n] - peak) / denom
        w_scr[n] = jnp.concatenate([weight, total, jnp.zeros((111, 128), F32)], axis=0).T
    total = w_scr[0][:, 16:17]
    high = total.astype(BF16).astype(F32)
    lane = lax.broadcasted_iota(jnp.int32, (128, 128), 1)
    totals = jnp.where(lane == 0, high, jnp.where(lane == 1, total - high, 0.0)).astype(BF16)

    for s in range(4):
        to = (info_ref[1] + s) % 4
        out_ref[pl.ds(to, 1), :, 768:896] = totals[None]

        @pl.when(seen[s])
        def _():
            for part in range(4):
                copy(s, part).wait()
            for r in range(0, 128, 16):
                weights = w_scr[s, r:r + 16, :]
                acc = buf[s, 0, r:r + 16, :].astype(F32) * weights[:, 0:1]
                for h in range(1, 16):
                    acc += buf[s, h, r:r + 16, :].astype(F32) * weights[:, h:h + 1]
                out_ref[pl.ds(to, 1), r:r + 16, 0:768] = acc.astype(BF16)[None]

        @pl.when(jnp.logical_not(seen[s]))
        def _():
            out_ref[pl.ds(to, 1), :, 0:768] = jnp.zeros((1, 128, 768), BF16)


def final_kernel(info_ref, got_ref, out_ref):
    slab, head = info_ref[0], info_ref[3]
    for y in range(4):
        rows = got_ref[4 * y].astype(F32)
        for h in range(1, 4):
            rows += got_ref[4 * y + h].astype(F32)
        total = rows[:, 768:769] + rows[:, 769:770]
        row = lax.broadcasted_iota(jnp.int32, (32, 1), 0)
        pos = (slab + head * 128 + y * 32 + row + 1).astype(F32)
        out_ref[y * 32:(y + 1) * 32, :] = rows[:, :768] * (pos / total)


def from_others(array):
    return [
        lax.ppermute(array, "x", [(i, (i - s) % NX) for i in range(NX)]) for s in (1, 2, 3)
    ]


def local(query_states, key_states, w_query, w_key, w_value, w_out, slab_start):
    x, zl, y = lax.axis_index("x"), lax.axis_index("zl"), lax.axis_index("y")
    head = lax.axis_index("zh") * NC + lax.axis_index("core")
    info = jnp.stack([slab_start[0], x, zl * NY + y, head]).astype(jnp.int32)

    params = pltpu.CompilerParams(vmem_limit_bytes=VMEM_LIMIT)
    vmem = pl.BlockSpec(memory_space=pltpu.VMEM)
    pay = pl.pallas_call(
        pack_kernel,
        out_shape=jax.ShapeDtypeStruct((4, 1280, 256), BF16),
        grid=(4,),
        in_specs=[
            pl.BlockSpec((256, 512), lambda i: (0, i)),
            pl.BlockSpec((512, 256), lambda i: (0, 0)),
            pl.BlockSpec((512, 256), lambda i: (i, 0)),
        ],
        out_specs=pl.BlockSpec((1, 1280, 256), lambda i: (i, 0, 0)),
        compiler_params=params,
        name="pack",
    )(w_query, query_states, w_out)
    got = lax.all_to_all(pay, "y", 0, 0, tiled=True)

    own_keys, own_values = pl.pallas_call(
        kv_kernel,
        out_shape=[jax.ShapeDtypeStruct((256, 768), BF16)] * 2,
        grid=(4,),
        in_specs=[
            pl.BlockSpec((768, 2048), lambda i: (0, i)),
            pl.BlockSpec((2048, 256), lambda i: (i, 0)),
            pl.BlockSpec((2048, 256), lambda i: (i, 0)),
        ],
        out_specs=[pl.BlockSpec((256, 768), lambda i: (0, 0))] * 2,
        scratch_shapes=[pltpu.VMEM((768, 512), F32)],
        compiler_params=params,
        name="project",
    )(key_states, w_key, w_value)
    got, *keys = lax.optimization_barrier((got, *from_others(own_keys)))
    keys = [own_keys] + keys
    parts = pl.pallas_call(
        partial_kernel,
        out_shape=jax.ShapeDtypeStruct((8, 64, 640), F32),
        in_specs=[vmem],
        out_specs=vmem,
        compiler_params=params,
        name="partial",
    )(got)
    parts = lax.all_to_all(parts, XZ, 0, 0, tiled=True)
    block = pl.pallas_call(
        sum_kernel,
        out_shape=jax.ShapeDtypeStruct((4, 8, 32, 512), BF16),
        in_specs=[vmem],
        out_specs=vmem,
        compiler_params=params,
        name="sum",
    )(parts)
    block = lax.all_to_all(block.reshape(32, 32, 512), CTX, 0, 0, tiled=True)
    block = block.reshape(8, 4, 32, 512)

    norms = pl.pallas_call(
        norm_kernel,
        out_shape=jax.ShapeDtypeStruct((4, 4, 768), F32),
        in_specs=[vmem, vmem],
        out_specs=vmem,
        compiler_params=params,
        name="norms",
    )(own_values, block)
    norms = [norms] + from_others(norms)

    q_spec = pl.BlockSpec((8, 1, 16, 512), lambda j, i: (0, j, 0, 0))
    k_spec = pl.BlockSpec((128, 768), lambda j, i: (j // 2, 0))
    n_spec = pl.BlockSpec((1, 4, 768), lambda j, i: (j, 0, 0))
    stat_spec = pl.BlockSpec((48, 128), lambda j, i: (0, 0))
    own_p, own_stats = pl.pallas_call(
        own_kernel,
        out_shape=(
            jax.ShapeDtypeStruct((16, 1, 128, 768), BF16),
            jax.ShapeDtypeStruct((48, 128), F32),
        ),
        grid_spec=pltpu.PrefetchScalarGridSpec(
            num_scalar_prefetch=1,
            grid=(4,),
            in_specs=[q_spec, k_spec, n_spec],
            out_specs=(pl.BlockSpec((4, 1, 128, 768), lambda j, i: (j, 0, 0, 0)), stat_spec),
            scratch_shapes=[pltpu.VMEM((1, 128, 128), F32)],
        ),
        compiler_params=params,
        name="own_scores",
    )(info, block, keys[0], norms[0])
    p, stats, peaks = pl.pallas_call(
        other_kernel,
        out_shape=(
            jax.ShapeDtypeStruct((16, 3, 128, 768), BF16),
            jax.ShapeDtypeStruct((8, 48, 128), F32),
            jax.ShapeDtypeStruct((4, 16, 128), F32),
        ),
        grid_spec=pltpu.PrefetchScalarGridSpec(
            num_scalar_prefetch=1,
            grid=(4,),
            in_specs=[q_spec, stat_spec] + [k_spec] * 3 + [n_spec] * 3,
            out_specs=(
                pl.BlockSpec((4, 3, 128, 768), lambda j, i: (j, 0, 0, 0)),
                pl.BlockSpec((8, 48, 128), lambda j, i: (0, 0, 0)),
                pl.BlockSpec((4, 16, 128), lambda j, i: (0, 0, 0)),
            ),
            scratch_shapes=[pltpu.VMEM((3, 128, 128), F32)],
        ),
        compiler_params=params,
        name="scores",
    )(info, block, own_stats, *keys[1:], *norms[1:])

    all_stats = lax.all_to_all(stats, ZY, 0, 0, tiled=True)

    smem, hbm = pl.BlockSpec(memory_space=pltpu.SMEM), pl.BlockSpec(memory_space=pl.ANY)
    pay = pl.pallas_call(
        map_kernel,
        out_shape=jax.ShapeDtypeStruct((4, 128, 896), BF16),
        in_specs=[smem, hbm, hbm, vmem, vmem],
        out_specs=vmem,
        scratch_shapes=[
            pltpu.VMEM((4, 16, 128, 768), BF16),
            pltpu.VMEM((4, 128, 128), F32),
            pltpu.SemaphoreType.DMA((4, 4)),
        ],
        compiler_params=params,
        name="weigh",
    )(info, own_p, p, peaks, all_stats)
    got = lax.all_to_all(pay.reshape(16, 32, 896), MAP, 0, 0, tiled=True)

    return pl.pallas_call(
        final_kernel,
        out_shape=jax.ShapeDtypeStruct((128, 768), F32),
        in_specs=[
            pl.BlockSpec(memory_space=pltpu.SMEM),
            pl.BlockSpec(memory_space=pltpu.VMEM),
        ],
        out_specs=pl.BlockSpec(memory_space=pltpu.VMEM),
        compiler_params=pltpu.CompilerParams(vmem_limit_bytes=VMEM_LIMIT),
        name="finish",
    )(info, got)


def solution(mesh):
    fine = Mesh(
        mesh.devices.reshape(NX, NZ, NY, NH, NC), ("x", "zl", "y", "zh", "core")
    )
    head = ("zh", "core")
    return jax.shard_map(
        local,
        mesh=fine,
        in_specs=(
            P(None, CTX),
            P(CTX, None),
            P(CTX, head),
            P(None, head),
            P(None, head),
            P(head, CTX),
            P(),
        ),
        out_specs=P(head, CTX),
        check_vma=False,
    )
```

```python
import jax
import jax.numpy as jnp
from jax import lax
from jax.experimental import pallas as pl
from jax.experimental.pallas import tpu as pltpu
from jax.sharding import Mesh, PartitionSpec as P

HEAD_DIM = 128
LOG2E = 1.4426950408889634
MASKED = -1e30
SCALE = HEAD_DIM ** -0.5 * LOG2E
NX, NZ, NY, NH, NC = 4, 2, 4, 2, 2
XZ, ZY, CTX, MAP = ("x", "zl"), ("zl", "y"), ("x", "zl", "y"), ("x", "zh", "core")
F32, BF16 = jnp.float32, jnp.bfloat16
VMEM_LIMIT = 56 * 1024 * 1024


def nn(a, b):
    return lax.dot_general(a, b, (((1,), (0,)), ((), ())), preferred_element_type=F32)


def nt(a, b):
    return lax.dot_general(a, b, (((1,), (1,)), ((), ())), preferred_element_type=F32)


def pack_kernel(wq_ref, qs_ref, wo_ref, out_ref):
    out_ref[0, 0:256, :] = wq_ref[:, 0:256]
    out_ref[0, 256:512, :] = wq_ref[:, 256:512]
    for block in range(4):
        for part in range(4):
            for half in range(2):
                src = ((block * 4 + part) * 2 + half) * 16
                dst = 512 + ((block * 2 + half) * 4 + part) * 16
                out_ref[0, dst:dst + 16, :] = qs_ref[src:src + 16, :]
    for h in range(4):
        rows = wo_ref[h * 128:(h + 1) * 128, :]
        at = 1024 + (h // 2) * 128
        out_ref[0, at:at + 128, (h % 2) * 128:(h % 2 + 1) * 128] = nt(rows, rows).astype(BF16)


def partial_kernel(got_ref, out_ref):
    for c in range(2):
        acc = jnp.zeros((512, 256), F32)
        for s in range(4):
            acc += nn(got_ref[s, 512:1024, :], got_ref[s, c * 256:(c + 1) * 256, :])
        out_ref[:, :, c * 256:(c + 1) * 256] = acc.reshape(8, 64, 256)
    for pair in range(2):
        gram = jnp.zeros((128, 256), F32)
        for s in range(4):
            gram += got_ref[s, 1024 + pair * 128:1024 + (pair + 1) * 128, :].astype(F32)
        for k in range(2):
            h = 2 * pair + k
            out_ref[2 * h, :, 512:640] = gram[:64, k * 128:(k + 1) * 128]
            out_ref[2 * h + 1, :, 512:640] = gram[64:, k * 128:(k + 1) * 128]


def sum_kernel(got_ref, out_ref):
    total = got_ref[0]
    for k in range(1, 8):
        total += got_ref[k]
    total = total.astype(BF16)
    gram = jnp.concatenate([total[b * 16:(b + 1) * 16, 512:640] for b in range(4)], axis=1)
    for part in range(4):
        for k in range(8):
            out_ref[part, k, 0:16, :] = total[part * 16:(part + 1) * 16, 0:512]
            out_ref[part, k, 16:32, :] = gram


def project_kernel(state_ref, w_ref, out_ref, acc):
    i = pl.program_id(0)
    part = nn(state_ref[...], w_ref[...])

    @pl.when(i == 0)
    def _():
        acc[...] = part

    @pl.when(i > 0)
    def _():
        acc[...] += part

    @pl.when(i == pl.num_programs(0) - 1)
    def _():
        out_ref[...] = acc[...].T.astype(BF16)


def project(states, weights, name):
    return pl.pallas_call(
        project_kernel,
        out_shape=jax.ShapeDtypeStruct((256, 768), BF16),
        grid=(4,),
        in_specs=[
            pl.BlockSpec((768, 2048), lambda i: (0, i)),
            pl.BlockSpec((2048, 256), lambda i: (i, 0)),
        ],
        out_specs=pl.BlockSpec((256, 768), lambda i: (0, 0)),
        scratch_shapes=[pltpu.VMEM((768, 256), F32)],
        compiler_params=pltpu.CompilerParams(vmem_limit_bytes=VMEM_LIMIT),
        name=name,
    )(states, weights)


def norm_kernel(value_ref, block_ref, out_ref):
    for h in range(16):
        gram = jnp.concatenate(
            [
                block_ref[2 * (h % 4) + half, h // 4, 16:32, b * 128:(b + 1) * 128]
                for half in range(2)
                for b in range(4)
            ],
            axis=0,
        )
        v = value_ref[(h // 8) * 128:(h // 8 + 1) * 128, :]
        quad = jnp.sum(nn(gram, v) * v.astype(F32), axis=0, keepdims=True)
        out_ref[h // 4, h % 4:h % 4 + 1, :] = jnp.sqrt(jnp.maximum(quad, 0.0) + 1e-6)


def tile_first(info_ref, s):
    return (((info_ref[1] + s) % 4) * 8 + info_ref[2]) * 768


def last_row(info_ref):
    return info_ref[0] + info_ref[1] * 32 + 3 * 128 + 31


def score_tiles(info_ref, q_ref, keys, norms, p_ref, acc, tiles):
    j = pl.program_id(0)
    slab, me = info_ref[0], info_ref[1]
    at = lax.broadcasted_iota(jnp.int32, (128, 128), 1)

    def scored(n, first, masked):
        k = keys[n][...]
        stat = acc[n]
        if masked:
            row = lax.broadcasted_iota(jnp.int32, (128, 1), 0)
            q_pos = slab + (row // 32) * 128 + me * 32 + row % 32
            seen = lax.broadcasted_iota(jnp.int32, (128, 768), 1) <= q_pos - first
        for i in range(4):
            q = q_ref[:, 0, :, i * 128:(i + 1) * 128].reshape(128, 128)
            scores = nn(q, k)
            if masked:
                scores = jnp.where(seen, scores, MASKED)
            peak = jnp.max(scores, axis=1, keepdims=True) * SCALE
            e = jnp.exp2(scores * SCALE - peak)
            p = e * norms[n][0, i:i + 1, :]
            h = 4 * j + i
            stat = jnp.where(at == h, peak, stat)
            stat = jnp.where(at == h + 16, jnp.sum(e, axis=1, keepdims=True), stat)
            stat = jnp.where(at == h + 32, jnp.sum(p, axis=1, keepdims=True), stat)
            p_ref[i, n] = p.astype(BF16)
        acc[n] = stat

    for n, s in enumerate(tiles):
        first = tile_first(info_ref, s)
        full = first + 767 <= slab + me * 32
        none = first > last_row(info_ref)

        @pl.when(full)
        def _():
            scored(n, first, False)

        @pl.when(jnp.logical_not(full) & jnp.logical_not(none))
        def _():
            scored(n, first, True)

        @pl.when(none)
        def _():
            acc[n] = jnp.where(at < 16, MASKED, 0.0)


def own_kernel(info_ref, q_ref, key_ref, norm_ref, p_ref, stat_ref, acc):
    score_tiles(info_ref, q_ref, [key_ref], [norm_ref], p_ref, acc, (0,))

    @pl.when(pl.program_id(0) == 3)
    def _():
        stat_ref[...] = acc[0].T[:48]


def other_kernel(info_ref, q_ref, own_ref, *refs):
    p_ref, stat_ref, peak_ref, acc = refs[6:]
    score_tiles(info_ref, q_ref, refs[0:3], refs[3:6], p_ref, acc, (1, 2, 3))

    @pl.when(pl.program_id(0) == 3)
    def _():
        stats = jnp.stack([own_ref[...]] + [acc[n].T[:48] for n in range(3)])
        peaks = stats[:, 0:16]
        peak = jnp.max(peaks, axis=0)
        factor = jnp.exp2(peaks - peak[None])
        denom = jnp.sum(stats[:, 16:32] * factor, axis=0)
        part = jnp.sum(stats[:, 32:48] * factor, axis=0)
        merged = jnp.concatenate([peak, denom, part], axis=0)
        stat_ref[...] = jnp.broadcast_to(merged[None], (8, 48, 128))
        peak_ref[...] = peaks


def map_kernel(info_ref, own_p_ref, p_ref, peak_ref, all_ref, out_ref, buf, w_scr, sems):
    seen = [tile_first(info_ref, s) <= last_row(info_ref) for s in range(4)]

    def copy(s, part):
        heads = pl.ds(part * 4, 4)
        src = own_p_ref.at[heads, 0] if s == 0 else p_ref.at[heads, s - 1]
        return pltpu.make_async_copy(src, buf.at[s, heads], sems.at[s, part])

    for s in range(4):
        @pl.when(seen[s])
        def _():
            for part in range(4):
                copy(s, part).start()

    peaks = all_ref[:, 0:16, :]
    peak = jnp.max(peaks, axis=0)
    factor = jnp.exp2(peaks - peak[None])
    denom = jnp.sum(all_ref[:, 16:32, :] * factor, axis=0)
    part_sum = jnp.sum(all_ref[:, 32:48, :] * factor, axis=0)
    total = jnp.sum(part_sum / denom, axis=0, keepdims=True)
    for n in range(4):
        weight = jnp.exp2(peak_ref[n] - peak) / denom
        w_scr[n] = jnp.concatenate([weight, total, jnp.zeros((111, 128), F32)], axis=0).T
    total = w_scr[0][:, 16:17]
    high = total.astype(BF16).astype(F32)
    lane = lax.broadcasted_iota(jnp.int32, (128, 128), 1)
    totals = jnp.where(lane == 0, high, jnp.where(lane == 1, total - high, 0.0)).astype(BF16)

    for s in range(4):
        to = (info_ref[1] + s) % 4
        out_ref[pl.ds(to, 1), :, 768:896] = totals[None]

        @pl.when(seen[s])
        def _():
            for part in range(4):
                copy(s, part).wait()
            for r in range(0, 128, 16):
                weights = w_scr[s, r:r + 16, :]
                acc = buf[s, 0, r:r + 16, :].astype(F32) * weights[:, 0:1]
                for h in range(1, 16):
                    acc += buf[s, h, r:r + 16, :].astype(F32) * weights[:, h:h + 1]
                out_ref[pl.ds(to, 1), r:r + 16, 0:768] = acc.astype(BF16)[None]

        @pl.when(jnp.logical_not(seen[s]))
        def _():
            out_ref[pl.ds(to, 1), :, 0:768] = jnp.zeros((1, 128, 768), BF16)


def final_kernel(info_ref, got_ref, out_ref):
    slab, head = info_ref[0], info_ref[3]
    for y in range(4):
        rows = got_ref[4 * y].astype(F32)
        for h in range(1, 4):
            rows += got_ref[4 * y + h].astype(F32)
        total = rows[:, 768:769] + rows[:, 769:770]
        row = lax.broadcasted_iota(jnp.int32, (32, 1), 0)
        pos = (slab + head * 128 + y * 32 + row + 1).astype(F32)
        out_ref[y * 32:(y + 1) * 32, :] = rows[:, :768] * (pos / total)


def from_others(array):
    return [
        lax.ppermute(array, "x", [(i, (i - s) % NX) for i in range(NX)]) for s in (1, 2, 3)
    ]


def local(query_states, key_states, w_query, w_key, w_value, w_out, slab_start):
    x, zl, y = lax.axis_index("x"), lax.axis_index("zl"), lax.axis_index("y")
    head = lax.axis_index("zh") * NC + lax.axis_index("core")
    info = jnp.stack([slab_start[0], x, zl * NY + y, head]).astype(jnp.int32)

    params = pltpu.CompilerParams(vmem_limit_bytes=VMEM_LIMIT)
    vmem = pl.BlockSpec(memory_space=pltpu.VMEM)
    pay = pl.pallas_call(
        pack_kernel,
        out_shape=jax.ShapeDtypeStruct((4, 1280, 256), BF16),
        grid=(4,),
        in_specs=[
            pl.BlockSpec((256, 512), lambda i: (0, i)),
            pl.BlockSpec((512, 256), lambda i: (0, 0)),
            pl.BlockSpec((512, 256), lambda i: (i, 0)),
        ],
        out_specs=pl.BlockSpec((1, 1280, 256), lambda i: (i, 0, 0)),
        compiler_params=params,
        name="pack",
    )(w_query, query_states, w_out)
    got = lax.all_to_all(pay, "y", 0, 0, tiled=True)

    own_keys = project(key_states, w_key, "project_keys")
    own_values = project(key_states, w_value, "project_values")
    got, info, own_values, *keys = lax.optimization_barrier(
        (got, info, own_values, *from_others(own_keys))
    )
    keys = [own_keys] + keys
    parts = pl.pallas_call(
        partial_kernel,
        out_shape=jax.ShapeDtypeStruct((8, 64, 640), F32),
        in_specs=[vmem],
        out_specs=vmem,
        compiler_params=params,
        name="partial",
    )(got)
    parts = lax.all_to_all(parts, XZ, 0, 0, tiled=True)
    block = pl.pallas_call(
        sum_kernel,
        out_shape=jax.ShapeDtypeStruct((4, 8, 32, 512), BF16),
        in_specs=[vmem],
        out_specs=vmem,
        compiler_params=params,
        name="sum",
    )(parts)
    block = lax.all_to_all(block.reshape(32, 32, 512), CTX, 0, 0, tiled=True)
    block = block.reshape(8, 4, 32, 512)

    norms = pl.pallas_call(
        norm_kernel,
        out_shape=jax.ShapeDtypeStruct((4, 4, 768), F32),
        in_specs=[vmem, vmem],
        out_specs=vmem,
        compiler_params=params,
        name="norms",
    )(own_values, block)
    norms = [norms] + from_others(norms)

    q_spec = pl.BlockSpec((8, 1, 16, 512), lambda j, i: (0, j, 0, 0))
    k_spec = pl.BlockSpec((128, 768), lambda j, i: (j // 2, 0))
    n_spec = pl.BlockSpec((1, 4, 768), lambda j, i: (j, 0, 0))
    stat_spec = pl.BlockSpec((48, 128), lambda j, i: (0, 0))
    own_p, own_stats = pl.pallas_call(
        own_kernel,
        out_shape=(
            jax.ShapeDtypeStruct((16, 1, 128, 768), BF16),
            jax.ShapeDtypeStruct((48, 128), F32),
        ),
        grid_spec=pltpu.PrefetchScalarGridSpec(
            num_scalar_prefetch=1,
            grid=(4,),
            in_specs=[q_spec, k_spec, n_spec],
            out_specs=(pl.BlockSpec((4, 1, 128, 768), lambda j, i: (j, 0, 0, 0)), stat_spec),
            scratch_shapes=[pltpu.VMEM((1, 128, 128), F32)],
        ),
        compiler_params=params,
        name="own_scores",
    )(info, block, keys[0], norms[0])
    p, stats, peaks = pl.pallas_call(
        other_kernel,
        out_shape=(
            jax.ShapeDtypeStruct((16, 3, 128, 768), BF16),
            jax.ShapeDtypeStruct((8, 48, 128), F32),
            jax.ShapeDtypeStruct((4, 16, 128), F32),
        ),
        grid_spec=pltpu.PrefetchScalarGridSpec(
            num_scalar_prefetch=1,
            grid=(4,),
            in_specs=[q_spec, stat_spec] + [k_spec] * 3 + [n_spec] * 3,
            out_specs=(
                pl.BlockSpec((4, 3, 128, 768), lambda j, i: (j, 0, 0, 0)),
                pl.BlockSpec((8, 48, 128), lambda j, i: (0, 0, 0)),
                pl.BlockSpec((4, 16, 128), lambda j, i: (0, 0, 0)),
            ),
            scratch_shapes=[pltpu.VMEM((3, 128, 128), F32)],
        ),
        compiler_params=params,
        name="scores",
    )(info, block, own_stats, *keys[1:], *norms[1:])

    all_stats = lax.all_to_all(stats, ZY, 0, 0, tiled=True)

    smem, hbm = pl.BlockSpec(memory_space=pltpu.SMEM), pl.BlockSpec(memory_space=pl.ANY)
    pay = pl.pallas_call(
        map_kernel,
        out_shape=jax.ShapeDtypeStruct((4, 128, 896), BF16),
        in_specs=[smem, hbm, hbm, vmem, vmem],
        out_specs=vmem,
        scratch_shapes=[
            pltpu.VMEM((4, 16, 128, 768), BF16),
            pltpu.VMEM((4, 128, 128), F32),
            pltpu.SemaphoreType.DMA((4, 4)),
        ],
        compiler_params=params,
        name="weigh",
    )(info, own_p, p, peaks, all_stats)
    got = lax.all_to_all(pay.reshape(16, 32, 896), MAP, 0, 0, tiled=True)

    return pl.pallas_call(
        final_kernel,
        out_shape=jax.ShapeDtypeStruct((128, 768), F32),
        in_specs=[
            pl.BlockSpec(memory_space=pltpu.SMEM),
            pl.BlockSpec(memory_space=pltpu.VMEM),
        ],
        out_specs=pl.BlockSpec(memory_space=pltpu.VMEM),
        compiler_params=pltpu.CompilerParams(vmem_limit_bytes=VMEM_LIMIT),
        name="finish",
    )(info, got)


def solution(mesh):
    fine = Mesh(
        mesh.devices.reshape(NX, NZ, NY, NH, NC), ("x", "zl", "y", "zh", "core")
    )
    head = ("zh", "core")
    return jax.shard_map(
        local,
        mesh=fine,
        in_specs=(
            P(None, CTX),
            P(CTX, None),
            P(CTX, head),
            P(None, head),
            P(None, head),
            P(head, CTX),
            P(),
        ),
        out_specs=P(head, CTX),
        check_vma=False,
    )
```

```python
import jax
import jax.numpy as jnp
from jax import lax
from jax.experimental import pallas as pl
from jax.experimental.pallas import tpu as pltpu
from jax.sharding import Mesh, PartitionSpec as P

HEAD_DIM = 128
LOG2E = 1.4426950408889634
MASKED = -1e30
SCALE = HEAD_DIM ** -0.5 * LOG2E
NX, NZ, NY, NH, NC = 4, 2, 4, 2, 2
XZ, ZY, CTX, MAP = ("x", "zl"), ("zl", "y"), ("x", "zl", "y"), ("x", "zh", "core")
F32, BF16 = jnp.float32, jnp.bfloat16
VMEM_LIMIT = 56 * 1024 * 1024


def nn(a, b):
    return lax.dot_general(a, b, (((1,), (0,)), ((), ())), preferred_element_type=F32)


def nt(a, b):
    return lax.dot_general(a, b, (((1,), (1,)), ((), ())), preferred_element_type=F32)


def pack_kernel(wq_ref, qs_ref, wo_ref, out_ref):
    out_ref[0, 0:256, :] = wq_ref[:, 0:256]
    out_ref[0, 256:512, :] = wq_ref[:, 256:512]
    for block in range(4):
        for part in range(4):
            for half in range(2):
                src = ((block * 4 + part) * 2 + half) * 16
                dst = 512 + ((block * 2 + half) * 4 + part) * 16
                out_ref[0, dst:dst + 16, :] = qs_ref[src:src + 16, :]
    for h in range(4):
        rows = wo_ref[h * 128:(h + 1) * 128, :]
        at = 1024 + (h // 2) * 128
        out_ref[0, at:at + 128, (h % 2) * 128:(h % 2 + 1) * 128] = nt(rows, rows).astype(BF16)


def partial_kernel(got_ref, out_ref, buf, sems):
    copies = [pltpu.make_async_copy(got_ref.at[s], buf.at[s], sems.at[s]) for s in range(4)]
    for copy in copies:
        copy.start()
    for s in range(4):
        copies[s].wait()
        parts = [
            nn(buf[s, 512:1024, :], buf[s, c * 256:(c + 1) * 256, :]).reshape(8, 64, 256)
            for c in range(2)
        ]
        grams = []
        for h in range(4):
            at = 1024 + (h // 2) * 128
            gram = buf[s, at:at + 128, (h % 2) * 128:(h % 2 + 1) * 128].astype(F32)
            grams.append(gram.reshape(2, 64, 128))
        part = jnp.concatenate(parts + [jnp.concatenate(grams, axis=0)], axis=2)
        out_ref[...] = part if s == 0 else out_ref[...] + part


def sum_kernel(got_ref, out_ref):
    total = got_ref[0]
    for k in range(1, 8):
        total += got_ref[k]
    total = total.astype(BF16)
    gram = jnp.concatenate([total[b * 16:(b + 1) * 16, 512:640] for b in range(4)], axis=1)
    for part in range(4):
        for k in range(8):
            out_ref[part, k, 0:16, :] = total[part * 16:(part + 1) * 16, 0:512]
            out_ref[part, k, 16:32, :] = gram


def project_kernel(state_ref, w_ref, out_ref, acc):
    i = pl.program_id(0)
    part = nn(state_ref[...], w_ref[...])

    @pl.when(i == 0)
    def _():
        acc[...] = part

    @pl.when(i > 0)
    def _():
        acc[...] += part

    @pl.when(i == pl.num_programs(0) - 1)
    def _():
        out_ref[...] = acc[...].T.astype(BF16)


def project(states, weights, name):
    return pl.pallas_call(
        project_kernel,
        out_shape=jax.ShapeDtypeStruct((256, 768), BF16),
        grid=(4,),
        in_specs=[
            pl.BlockSpec((768, 2048), lambda i: (0, i)),
            pl.BlockSpec((2048, 256), lambda i: (i, 0)),
        ],
        out_specs=pl.BlockSpec((256, 768), lambda i: (0, 0)),
        scratch_shapes=[pltpu.VMEM((768, 256), F32)],
        compiler_params=pltpu.CompilerParams(vmem_limit_bytes=VMEM_LIMIT),
        name=name,
    )(states, weights)


def norm_kernel(value_ref, block_ref, out_ref):
    for h in range(16):
        gram = jnp.concatenate(
            [
                block_ref[2 * (h % 4) + half, h // 4, 16:32, b * 128:(b + 1) * 128]
                for half in range(2)
                for b in range(4)
            ],
            axis=0,
        )
        v = value_ref[(h // 8) * 128:(h // 8 + 1) * 128, :]
        quad = jnp.sum(nn(gram, v) * v.astype(F32), axis=0, keepdims=True)
        out_ref[h // 4, h % 4:h % 4 + 1, :] = jnp.sqrt(jnp.maximum(quad, 0.0) + 1e-6)


def tile_first(info_ref, s):
    return (((info_ref[1] + s) % 4) * 8 + info_ref[2]) * 768


def last_row(info_ref):
    return info_ref[0] + info_ref[1] * 32 + 3 * 128 + 31


def score_tiles(info_ref, block_ref, keys, norms, p_ref, buf, acc, sems, tiles):
    slab, me = info_ref[0], info_ref[1]
    at = lax.broadcasted_iota(jnp.int32, (128, 128), 1)
    firsts = [tile_first(info_ref, s) for s in tiles]
    unseen = [first > last_row(info_ref) for first in firsts]

    def copy(j, n):
        heads = pl.ds(4 * j, 4)
        return pltpu.make_async_copy(buf.at[heads, n], p_ref.at[heads, n], sems.at[j, n])

    def scored(j, n, masked):
        k = keys[n][pl.ds(pl.multiple_of((j // 2) * 128, 128), 128), :]
        stat = acc[n]
        if masked:
            row = lax.broadcasted_iota(jnp.int32, (128, 1), 0)
            q_pos = slab + (row // 32) * 128 + me * 32 + row % 32
            seen = lax.broadcasted_iota(jnp.int32, (128, 768), 1) <= q_pos - firsts[n]
        for i in range(4):
            q = block_ref[:, j, 0:16, i * 128:(i + 1) * 128].reshape(128, 128)
            scores = nn(q, k)
            if masked:
                scores = jnp.where(seen, scores, MASKED)
            peak = jnp.max(scores, axis=1, keepdims=True) * SCALE
            e = jnp.exp2(scores * SCALE - peak)
            p = e * norms[n][j, i:i + 1, :]
            h = 4 * j + i
            stat = jnp.where(at == h, peak, stat)
            stat = jnp.where(at == h + 16, jnp.sum(e, axis=1, keepdims=True), stat)
            stat = jnp.where(at == h + 32, jnp.sum(p, axis=1, keepdims=True), stat)
            buf[h, n] = p.astype(BF16)
        acc[n] = stat
        copy(j, n).start()

    for n in range(len(tiles)):
        acc[n] = jnp.where(at < 16, MASKED, 0.0)

    def heads(j, carry):
        for n in range(len(tiles)):
            full = firsts[n] + 767 <= slab + me * 32

            @pl.when(full)
            def _():
                scored(j, n, False)

            @pl.when(jnp.logical_not(full) & jnp.logical_not(unseen[n]))
            def _():
                scored(j, n, True)
        return carry

    lax.fori_loop(0, 4, heads, 0)

    def finish():
        for n in range(len(tiles)):
            @pl.when(jnp.logical_not(unseen[n]))
            def _():
                for j in range(4):
                    copy(j, n).wait()

    return finish


def own_kernel(info_ref, block_ref, key_ref, norm_ref, p_ref, stat_ref, buf, acc, sems):
    finish = score_tiles(info_ref, block_ref, [key_ref], [norm_ref], p_ref, buf, acc, sems, (0,))
    stat_ref[...] = acc[0].T[:48]
    finish()


def other_kernel(info_ref, block_ref, own_ref, *refs):
    p_ref, stat_ref, peak_ref, buf, acc, sems = refs[6:]
    finish = score_tiles(
        info_ref, block_ref, refs[0:3], refs[3:6], p_ref, buf, acc, sems, (1, 2, 3)
    )
    stats = jnp.stack([own_ref[...]] + [acc[n].T[:48] for n in range(3)])
    peaks = stats[:, 0:16]
    peak = jnp.max(peaks, axis=0)
    factor = jnp.exp2(peaks - peak[None])
    denom = jnp.sum(stats[:, 16:32] * factor, axis=0)
    part = jnp.sum(stats[:, 32:48] * factor, axis=0)
    merged = jnp.concatenate([peak, denom, part], axis=0)
    stat_ref[...] = jnp.broadcast_to(merged[None], (8, 48, 128))
    peak_ref[...] = peaks
    finish()


def map_kernel(info_ref, own_p_ref, p_ref, peak_ref, all_ref, out_ref, buf, w_scr, sems):
    seen = [tile_first(info_ref, s) <= last_row(info_ref) for s in range(4)]

    def copy(s, part):
        heads = pl.ds(part * 4, 4)
        src = own_p_ref.at[heads, 0] if s == 0 else p_ref.at[heads, s - 1]
        return pltpu.make_async_copy(src, buf.at[s, heads], sems.at[s, part])

    for s in range(4):
        @pl.when(seen[s])
        def _():
            for part in range(4):
                copy(s, part).start()

    peaks = all_ref[:, 0:16, :]
    peak = jnp.max(peaks, axis=0)
    factor = jnp.exp2(peaks - peak[None])
    denom = jnp.sum(all_ref[:, 16:32, :] * factor, axis=0)
    part_sum = jnp.sum(all_ref[:, 32:48, :] * factor, axis=0)
    total = jnp.sum(part_sum / denom, axis=0, keepdims=True)
    for n in range(4):
        weight = jnp.exp2(peak_ref[n] - peak) / denom
        w_scr[n] = jnp.concatenate([weight, total, jnp.zeros((111, 128), F32)], axis=0).T
    total = w_scr[0][:, 16:17]
    high = total.astype(BF16).astype(F32)
    lane = lax.broadcasted_iota(jnp.int32, (128, 128), 1)
    totals = jnp.where(lane == 0, high, jnp.where(lane == 1, total - high, 0.0)).astype(BF16)

    for s in range(4):
        to = (info_ref[1] + s) % 4
        out_ref[pl.ds(to, 1), :, 768:896] = totals[None]

        @pl.when(seen[s])
        def _():
            for part in range(4):
                copy(s, part).wait()
            for r in range(0, 128, 16):
                weights = w_scr[s, r:r + 16, :]
                acc = buf[s, 0, r:r + 16, :].astype(F32) * weights[:, 0:1]
                for h in range(1, 16):
                    acc += buf[s, h, r:r + 16, :].astype(F32) * weights[:, h:h + 1]
                out_ref[pl.ds(to, 1), r:r + 16, 0:768] = acc.astype(BF16)[None]

        @pl.when(jnp.logical_not(seen[s]))
        def _():
            out_ref[pl.ds(to, 1), :, 0:768] = jnp.zeros((1, 128, 768), BF16)


def final_kernel(info_ref, got_ref, out_ref):
    slab, head = info_ref[0], info_ref[3]
    for y in range(4):
        rows = got_ref[4 * y].astype(F32)
        for h in range(1, 4):
            rows += got_ref[4 * y + h].astype(F32)
        total = rows[:, 768:769] + rows[:, 769:770]
        row = lax.broadcasted_iota(jnp.int32, (32, 1), 0)
        pos = (slab + head * 128 + y * 32 + row + 1).astype(F32)
        out_ref[y * 32:(y + 1) * 32, :] = rows[:, :768] * (pos / total)


def from_others(array):
    return [
        lax.ppermute(array, "x", [(i, (i - s) % NX) for i in range(NX)]) for s in (1, 2, 3)
    ]


def local(query_states, key_states, w_query, w_key, w_value, w_out, slab_start):
    x, zl, y = lax.axis_index("x"), lax.axis_index("zl"), lax.axis_index("y")
    head = lax.axis_index("zh") * NC + lax.axis_index("core")
    info = jnp.stack([slab_start[0], x, zl * NY + y, head]).astype(jnp.int32)

    params = pltpu.CompilerParams(vmem_limit_bytes=VMEM_LIMIT)
    vmem = pl.BlockSpec(memory_space=pltpu.VMEM)
    smem, hbm = pl.BlockSpec(memory_space=pltpu.SMEM), pl.BlockSpec(memory_space=pl.ANY)
    pay = pl.pallas_call(
        pack_kernel,
        out_shape=jax.ShapeDtypeStruct((4, 1280, 256), BF16),
        grid=(4,),
        in_specs=[
            pl.BlockSpec((256, 512), lambda i: (0, i)),
            pl.BlockSpec((512, 256), lambda i: (0, 0)),
            pl.BlockSpec((512, 256), lambda i: (i, 0)),
        ],
        out_specs=pl.BlockSpec((1, 1280, 256), lambda i: (i, 0, 0)),
        compiler_params=params,
        name="pack",
    )(w_query, query_states, w_out)
    got = lax.all_to_all(pay, "y", 0, 0, tiled=True)

    own_keys = project(key_states, w_key, "project_keys")
    own_values = project(key_states, w_value, "project_values")
    got, info, own_values, *keys = lax.optimization_barrier(
        (got, info, own_values, *from_others(own_keys))
    )
    keys = [own_keys] + keys
    parts = pl.pallas_call(
        partial_kernel,
        out_shape=jax.ShapeDtypeStruct((8, 64, 640), F32),
        in_specs=[hbm],
        out_specs=vmem,
        scratch_shapes=[pltpu.VMEM((4, 1280, 256), BF16), pltpu.SemaphoreType.DMA((4,))],
        compiler_params=params,
        name="partial",
    )(got)
    parts = lax.all_to_all(parts, XZ, 0, 0, tiled=True)
    block = pl.pallas_call(
        sum_kernel,
        out_shape=jax.ShapeDtypeStruct((4, 8, 32, 512), BF16),
        in_specs=[vmem],
        out_specs=vmem,
        compiler_params=params,
        name="sum",
    )(parts)
    block = lax.all_to_all(block.reshape(32, 32, 512), CTX, 0, 0, tiled=True)
    block = block.reshape(8, 4, 32, 512)

    norms = pl.pallas_call(
        norm_kernel,
        out_shape=jax.ShapeDtypeStruct((4, 4, 768), F32),
        in_specs=[vmem, vmem],
        out_specs=vmem,
        compiler_params=params,
        name="norms",
    )(own_values, block)
    norms = [norms] + from_others(norms)


    def scores_call(kernel, count, name, shapes, *operands):
        return pl.pallas_call(
            kernel,
            out_shape=[jax.ShapeDtypeStruct((16, count, 128, 768), BF16)]
            + [jax.ShapeDtypeStruct(shape, F32) for shape in shapes],
            in_specs=[smem] + [vmem] * len(operands),
            out_specs=[hbm] + [vmem] * len(shapes),
            scratch_shapes=[
                pltpu.VMEM((16, count, 128, 768), BF16),
                pltpu.VMEM((count, 128, 128), F32),
                pltpu.SemaphoreType.DMA((4, count)),
            ],
            compiler_params=params,
            name=name,
        )(info, *operands)

    own_p, own_stats = scores_call(
        own_kernel, 1, "own_scores", [(48, 128)], block, keys[0], norms[0]
    )
    p, stats, peaks = scores_call(
        other_kernel, 3, "scores", [(8, 48, 128), (4, 16, 128)],
        block, own_stats, *keys[1:], *norms[1:],
    )

    all_stats = lax.all_to_all(stats, ZY, 0, 0, tiled=True)

    pay = pl.pallas_call(
        map_kernel,
        out_shape=jax.ShapeDtypeStruct((4, 128, 896), BF16),
        in_specs=[smem, hbm, hbm, vmem, vmem],
        out_specs=vmem,
        scratch_shapes=[
            pltpu.VMEM((4, 16, 128, 768), BF16),
            pltpu.VMEM((4, 128, 128), F32),
            pltpu.SemaphoreType.DMA((4, 4)),
        ],
        compiler_params=params,
        name="weigh",
    )(info, own_p, p, peaks, all_stats)
    got = lax.all_to_all(pay.reshape(16, 32, 896), MAP, 0, 0, tiled=True)

    return pl.pallas_call(
        final_kernel,
        out_shape=jax.ShapeDtypeStruct((128, 768), F32),
        in_specs=[
            pl.BlockSpec(memory_space=pltpu.SMEM),
            pl.BlockSpec(memory_space=pltpu.VMEM),
        ],
        out_specs=pl.BlockSpec(memory_space=pltpu.VMEM),
        compiler_params=pltpu.CompilerParams(vmem_limit_bytes=VMEM_LIMIT),
        name="finish",
    )(info, got)


def solution(mesh):
    fine = Mesh(
        mesh.devices.reshape(NX, NZ, NY, NH, NC), ("x", "zl", "y", "zh", "core")
    )
    head = ("zh", "core")
    return jax.shard_map(
        local,
        mesh=fine,
        in_specs=(
            P(None, CTX),
            P(CTX, None),
            P(CTX, head),
            P(None, head),
            P(None, head),
            P(head, CTX),
            P(),
        ),
        out_specs=P(head, CTX),
        check_vma=False,
    )
```

```python
import jax
import jax.numpy as jnp
from jax import lax
from jax.experimental import pallas as pl
from jax.experimental.pallas import tpu as pltpu
from jax.sharding import Mesh, PartitionSpec as P

HEAD_DIM = 128
LOG2E = 1.4426950408889634
MASKED = -1e30
SCALE = HEAD_DIM ** -0.5 * LOG2E
NX, NZ, NY, NH, NC = 4, 2, 4, 2, 2
XZ, ZY, CTX, MAP = ("x", "zl"), ("zl", "y"), ("x", "zl", "y"), ("x", "zh", "core")
F32, BF16 = jnp.float32, jnp.bfloat16
VMEM_LIMIT = 56 * 1024 * 1024


def nn(a, b):
    return lax.dot_general(a, b, (((1,), (0,)), ((), ())), preferred_element_type=F32)


def nt(a, b):
    return lax.dot_general(a, b, (((1,), (1,)), ((), ())), preferred_element_type=F32)


def pack_kernel(wq_ref, qs_ref, wo_ref, out_ref, buf, qs_buf, wo_buf, qs_sem, wq_sems, wo_sems, sems):
    rows_in = pltpu.make_async_copy(qs_ref, qs_buf, qs_sem)
    rows_in.start()
    columns_in, heads_in = [], []
    for i in range(4):
        heads_in.append(
            pltpu.make_async_copy(wo_ref.at[pl.ds(i * 512, 512)], wo_buf.at[i], wo_sems.at[i])
        )
        heads_in[i].start()
        for c in range(2):
            copy = pltpu.make_async_copy(
                wq_ref.at[:, pl.ds((2 * i + c) * 256, 256)],
                buf.at[i, pl.ds(c * 256, 256)],
                wq_sems.at[i, c],
            )
            copy.start()
            columns_in.append(copy)
    rows_in.wait()
    copies_out = []
    for i in range(4):
        for block in range(4):
            for part in range(4):
                for half in range(2):
                    src = ((block * 4 + part) * 2 + half) * 16
                    dst = 512 + ((block * 2 + half) * 4 + part) * 16
                    buf[i, dst:dst + 16, :] = qs_buf[src:src + 16, :]
        heads_in[i].wait()
        for h in range(4):
            rows = wo_buf[i, h * 128:(h + 1) * 128, :]
            at = 1024 + (h // 2) * 128
            buf[i, at:at + 128, (h % 2) * 128:(h % 2 + 1) * 128] = nt(rows, rows).astype(BF16)
        columns_in[2 * i].wait()
        columns_in[2 * i + 1].wait()
        copies_out.append(pltpu.make_async_copy(buf.at[i], out_ref.at[i], sems.at[i]))
        copies_out[i].start()
    for copy in copies_out:
        copy.wait()


def partial_kernel(got_ref, out_ref, buf, sems):
    copies = [pltpu.make_async_copy(got_ref.at[s], buf.at[s], sems.at[s]) for s in range(4)]
    for copy in copies:
        copy.start()
    for s in range(4):
        copies[s].wait()
        parts = [
            nn(buf[s, 512:1024, :], buf[s, c * 256:(c + 1) * 256, :]).reshape(8, 64, 256)
            for c in range(2)
        ]
        grams = []
        for h in range(4):
            at = 1024 + (h // 2) * 128
            gram = buf[s, at:at + 128, (h % 2) * 128:(h % 2 + 1) * 128].astype(F32)
            grams.append(gram.reshape(2, 64, 128))
        part = jnp.concatenate(parts + [jnp.concatenate(grams, axis=0)], axis=2)
        out_ref[...] = part if s == 0 else out_ref[...] + part


def sum_kernel(got_ref, out_ref):
    total = got_ref[0]
    for k in range(1, 8):
        total += got_ref[k]
    total = total.astype(BF16)
    gram = jnp.concatenate([total[b * 16:(b + 1) * 16, 512:640] for b in range(4)], axis=1)
    for part in range(4):
        for k in range(8):
            out_ref[part, k, 0:16, :] = total[part * 16:(part + 1) * 16, 0:512]
            out_ref[part, k, 16:32, :] = gram


def project_kernel(state_ref, w_ref, out_ref, acc):
    i = pl.program_id(0)
    part = nn(state_ref[...], w_ref[...])

    @pl.when(i == 0)
    def _():
        acc[...] = part

    @pl.when(i > 0)
    def _():
        acc[...] += part

    @pl.when(i == pl.num_programs(0) - 1)
    def _():
        out_ref[...] = acc[...].T.astype(BF16)


def project(states, weights, name):
    return pl.pallas_call(
        project_kernel,
        out_shape=jax.ShapeDtypeStruct((256, 768), BF16),
        grid=(4,),
        in_specs=[
            pl.BlockSpec((768, 2048), lambda i: (0, i)),
            pl.BlockSpec((2048, 256), lambda i: (i, 0)),
        ],
        out_specs=pl.BlockSpec((256, 768), lambda i: (0, 0)),
        scratch_shapes=[pltpu.VMEM((768, 256), F32)],
        compiler_params=pltpu.CompilerParams(vmem_limit_bytes=VMEM_LIMIT),
        name=name,
    )(states, weights)


def norm_kernel(value_ref, block_ref, out_ref):
    for h in range(16):
        gram = jnp.concatenate(
            [
                block_ref[2 * (h % 4) + half, h // 4, 16:32, b * 128:(b + 1) * 128]
                for half in range(2)
                for b in range(4)
            ],
            axis=0,
        )
        v = value_ref[(h // 8) * 128:(h // 8 + 1) * 128, :]
        quad = jnp.sum(nn(gram, v) * v.astype(F32), axis=0, keepdims=True)
        out_ref[h // 4, h % 4:h % 4 + 1, :] = jnp.sqrt(jnp.maximum(quad, 0.0) + 1e-6)


def tile_first(info_ref, s):
    return (((info_ref[1] + s) % 4) * 8 + info_ref[2]) * 768


def last_row(info_ref):
    return info_ref[0] + info_ref[1] * 32 + 3 * 128 + 31


def score_tiles(info_ref, block_ref, keys, norms, p_ref, buf, acc, sems, tiles):
    slab, me = info_ref[0], info_ref[1]
    at = lax.broadcasted_iota(jnp.int32, (128, 128), 1)
    firsts = [tile_first(info_ref, s) for s in tiles]
    unseen = [first > last_row(info_ref) for first in firsts]

    def copy(j, n):
        heads = pl.ds(4 * j, 4)
        return pltpu.make_async_copy(buf.at[heads, n], p_ref.at[heads, n], sems.at[j, n])

    def scored(j, n, masked):
        k = keys[n][pl.ds(pl.multiple_of((j // 2) * 128, 128), 128), :]
        stat = acc[n]
        if masked:
            row = lax.broadcasted_iota(jnp.int32, (128, 1), 0)
            q_pos = slab + (row // 32) * 128 + me * 32 + row % 32
            seen = lax.broadcasted_iota(jnp.int32, (128, 768), 1) <= q_pos - firsts[n]
        for i in range(4):
            q = block_ref[:, j, 0:16, i * 128:(i + 1) * 128].reshape(128, 128)
            scores = nn(q, k)
            if masked:
                scores = jnp.where(seen, scores, MASKED)
            peak = jnp.max(scores, axis=1, keepdims=True) * SCALE
            e = jnp.exp2(scores * SCALE - peak)
            p = e * norms[n][j, i:i + 1, :]
            h = 4 * j + i
            stat = jnp.where(at == h, peak, stat)
            stat = jnp.where(at == h + 16, jnp.sum(e, axis=1, keepdims=True), stat)
            stat = jnp.where(at == h + 32, jnp.sum(p, axis=1, keepdims=True), stat)
            buf[h, n] = p.astype(BF16)
        acc[n] = stat
        copy(j, n).start()

    for n in range(len(tiles)):
        acc[n] = jnp.where(at < 16, MASKED, 0.0)

    def heads(j, carry):
        for n in range(len(tiles)):
            full = firsts[n] + 767 <= slab + me * 32

            @pl.when(full)
            def _():
                scored(j, n, False)

            @pl.when(jnp.logical_not(full) & jnp.logical_not(unseen[n]))
            def _():
                scored(j, n, True)
        return carry

    lax.fori_loop(0, 4, heads, 0)

    def finish():
        for n in range(len(tiles)):
            @pl.when(jnp.logical_not(unseen[n]))
            def _():
                for j in range(4):
                    copy(j, n).wait()

    return finish


def own_kernel(info_ref, block_ref, key_ref, norm_ref, p_ref, stat_ref, buf, acc, sems):
    finish = score_tiles(info_ref, block_ref, [key_ref], [norm_ref], p_ref, buf, acc, sems, (0,))
    stat_ref[...] = acc[0].T[:48]
    finish()


def other_kernel(info_ref, block_ref, own_ref, *refs):
    p_ref, stat_ref, peak_ref, buf, acc, sems = refs[6:]
    finish = score_tiles(
        info_ref, block_ref, refs[0:3], refs[3:6], p_ref, buf, acc, sems, (1, 2, 3)
    )
    stats = jnp.stack([own_ref[...]] + [acc[n].T[:48] for n in range(3)])
    peaks = stats[:, 0:16]
    peak = jnp.max(peaks, axis=0)
    factor = jnp.exp2(peaks - peak[None])
    denom = jnp.sum(stats[:, 16:32] * factor, axis=0)
    part = jnp.sum(stats[:, 32:48] * factor, axis=0)
    merged = jnp.concatenate([peak, denom, part], axis=0)
    stat_ref[...] = jnp.broadcast_to(merged[None], (8, 48, 128))
    peak_ref[...] = peaks
    finish()


def map_kernel(info_ref, own_p_ref, p_ref, peak_ref, all_ref, out_ref, buf, w_scr, sems):
    seen = [tile_first(info_ref, s) <= last_row(info_ref) for s in range(4)]

    def copy(s, part):
        heads = pl.ds(part * 4, 4)
        src = own_p_ref.at[heads, 0] if s == 0 else p_ref.at[heads, s - 1]
        return pltpu.make_async_copy(src, buf.at[s, heads], sems.at[s, part])

    for s in range(4):
        @pl.when(seen[s])
        def _():
            for part in range(4):
                copy(s, part).start()

    peaks = all_ref[:, 0:16, :]
    peak = jnp.max(peaks, axis=0)
    factor = jnp.exp2(peaks - peak[None])
    denom = jnp.sum(all_ref[:, 16:32, :] * factor, axis=0)
    part_sum = jnp.sum(all_ref[:, 32:48, :] * factor, axis=0)
    total = jnp.sum(part_sum / denom, axis=0, keepdims=True)
    for n in range(4):
        weight = jnp.exp2(peak_ref[n] - peak) / denom
        w_scr[n] = jnp.concatenate([weight, total, jnp.zeros((111, 128), F32)], axis=0).T
    total = w_scr[0][:, 16:17]
    high = total.astype(BF16).astype(F32)
    lane = lax.broadcasted_iota(jnp.int32, (128, 128), 1)
    totals = jnp.where(lane == 0, high, jnp.where(lane == 1, total - high, 0.0)).astype(BF16)

    for s in range(4):
        to = (info_ref[1] + s) % 4
        out_ref[pl.ds(to, 1), :, 768:896] = totals[None]

        @pl.when(seen[s])
        def _():
            for part in range(4):
                copy(s, part).wait()
            for r in range(0, 128, 16):
                weights = w_scr[s, r:r + 16, :]
                acc = buf[s, 0, r:r + 16, :].astype(F32) * weights[:, 0:1]
                for h in range(1, 16):
                    acc += buf[s, h, r:r + 16, :].astype(F32) * weights[:, h:h + 1]
                out_ref[pl.ds(to, 1), r:r + 16, 0:768] = acc.astype(BF16)[None]

        @pl.when(jnp.logical_not(seen[s]))
        def _():
            out_ref[pl.ds(to, 1), :, 0:768] = jnp.zeros((1, 128, 768), BF16)


def final_kernel(info_ref, got_ref, out_ref):
    slab, head = info_ref[0], info_ref[3]
    for y in range(4):
        rows = got_ref[4 * y].astype(F32)
        for h in range(1, 4):
            rows += got_ref[4 * y + h].astype(F32)
        total = rows[:, 768:769] + rows[:, 769:770]
        row = lax.broadcasted_iota(jnp.int32, (32, 1), 0)
        pos = (slab + head * 128 + y * 32 + row + 1).astype(F32)
        out_ref[y * 32:(y + 1) * 32, :] = rows[:, :768] * (pos / total)


def from_others(array):
    return [
        lax.ppermute(array, "x", [(i, (i - s) % NX) for i in range(NX)]) for s in (1, 2, 3)
    ]


def local(query_states, key_states, w_query, w_key, w_value, w_out, slab_start):
    x, zl, y = lax.axis_index("x"), lax.axis_index("zl"), lax.axis_index("y")
    head = lax.axis_index("zh") * NC + lax.axis_index("core")
    info = jnp.stack([slab_start[0], x, zl * NY + y, head]).astype(jnp.int32)

    params = pltpu.CompilerParams(vmem_limit_bytes=VMEM_LIMIT)
    vmem = pl.BlockSpec(memory_space=pltpu.VMEM)
    smem, hbm = pl.BlockSpec(memory_space=pltpu.SMEM), pl.BlockSpec(memory_space=pl.ANY)
    pay = pl.pallas_call(
        pack_kernel,
        out_shape=jax.ShapeDtypeStruct((4, 1280, 256), BF16),
        in_specs=[hbm] * 3,
        out_specs=hbm,
        scratch_shapes=[
            pltpu.VMEM((4, 1280, 256), BF16),
            pltpu.VMEM((512, 256), BF16),
            pltpu.VMEM((4, 512, 256), BF16),
            pltpu.SemaphoreType.DMA,
            pltpu.SemaphoreType.DMA((4, 2)),
            pltpu.SemaphoreType.DMA((4,)),
            pltpu.SemaphoreType.DMA((4,)),
        ],
        compiler_params=params,
        name="pack",
    )(w_query, query_states, w_out)
    got = lax.all_to_all(pay, "y", 0, 0, tiled=True)

    own_keys = project(key_states, w_key, "project_keys")
    own_values = project(key_states, w_value, "project_values")
    got, info, own_values, *keys = lax.optimization_barrier(
        (got, info, own_values, *from_others(own_keys))
    )
    keys = [own_keys] + keys
    parts = pl.pallas_call(
        partial_kernel,
        out_shape=jax.ShapeDtypeStruct((8, 64, 640), F32),
        in_specs=[hbm],
        out_specs=vmem,
        scratch_shapes=[pltpu.VMEM((4, 1280, 256), BF16), pltpu.SemaphoreType.DMA((4,))],
        compiler_params=params,
        name="partial",
    )(got)
    parts = lax.all_to_all(parts, XZ, 0, 0, tiled=True)
    block = pl.pallas_call(
        sum_kernel,
        out_shape=jax.ShapeDtypeStruct((4, 8, 32, 512), BF16),
        in_specs=[vmem],
        out_specs=vmem,
        compiler_params=params,
        name="sum",
    )(parts)
    block = lax.all_to_all(block.reshape(32, 32, 512), CTX, 0, 0, tiled=True)
    block = block.reshape(8, 4, 32, 512)

    norms = pl.pallas_call(
        norm_kernel,
        out_shape=jax.ShapeDtypeStruct((4, 4, 768), F32),
        in_specs=[vmem, vmem],
        out_specs=vmem,
        compiler_params=params,
        name="norms",
    )(own_values, block)
    norms = [norms] + from_others(norms)


    def scores_call(kernel, count, name, shapes, *operands):
        return pl.pallas_call(
            kernel,
            out_shape=[jax.ShapeDtypeStruct((16, count, 128, 768), BF16)]
            + [jax.ShapeDtypeStruct(shape, F32) for shape in shapes],
            in_specs=[smem] + [vmem] * len(operands),
            out_specs=[hbm] + [vmem] * len(shapes),
            scratch_shapes=[
                pltpu.VMEM((16, count, 128, 768), BF16),
                pltpu.VMEM((count, 128, 128), F32),
                pltpu.SemaphoreType.DMA((4, count)),
            ],
            compiler_params=params,
            name=name,
        )(info, *operands)

    own_p, own_stats = scores_call(
        own_kernel, 1, "own_scores", [(48, 128)], block, keys[0], norms[0]
    )
    p, stats, peaks = scores_call(
        other_kernel, 3, "scores", [(8, 48, 128), (4, 16, 128)],
        block, own_stats, *keys[1:], *norms[1:],
    )

    all_stats = lax.all_to_all(stats, ZY, 0, 0, tiled=True)

    pay = pl.pallas_call(
        map_kernel,
        out_shape=jax.ShapeDtypeStruct((4, 128, 896), BF16),
        in_specs=[smem, hbm, hbm, vmem, vmem],
        out_specs=vmem,
        scratch_shapes=[
            pltpu.VMEM((4, 16, 128, 768), BF16),
            pltpu.VMEM((4, 128, 128), F32),
            pltpu.SemaphoreType.DMA((4, 4)),
        ],
        compiler_params=params,
        name="weigh",
    )(info, own_p, p, peaks, all_stats)
    got = lax.all_to_all(pay.reshape(16, 32, 896), MAP, 0, 0, tiled=True)

    return pl.pallas_call(
        final_kernel,
        out_shape=jax.ShapeDtypeStruct((128, 768), F32),
        in_specs=[
            pl.BlockSpec(memory_space=pltpu.SMEM),
            pl.BlockSpec(memory_space=pltpu.VMEM),
        ],
        out_specs=pl.BlockSpec(memory_space=pltpu.VMEM),
        compiler_params=pltpu.CompilerParams(vmem_limit_bytes=VMEM_LIMIT),
        name="finish",
    )(info, got)


def solution(mesh):
    fine = Mesh(
        mesh.devices.reshape(NX, NZ, NY, NH, NC), ("x", "zl", "y", "zh", "core")
    )
    head = ("zh", "core")
    return jax.shard_map(
        local,
        mesh=fine,
        in_specs=(
            P(None, CTX),
            P(CTX, None),
            P(CTX, head),
            P(None, head),
            P(None, head),
            P(head, CTX),
            P(),
        ),
        out_specs=P(head, CTX),
        check_vma=False,
    )
```
